32 devices in a mesh: case: 2 (over y), wall: 4 (over z), azim: 4 (over x, core).
Axes of the slice: x: 2, y: 2, z: 4, core: 2. Of those that a mesh axis runs over, the one named last changes fastest.
Arguments:
- state: float32 [12, 2, 32, 512], P(None, 'case', 'wall', 'azim'), parts along dimension 1, may hold values from 0.5 to 1.5
- courant: float32 [2, 32, 512], P('case', 'wall', 'azim'), parts along dimension 0, may hold values from -0.6 to 0.6
- cross_sections: float32 [64], replicated, may hold values from 0.02 to 0.6
- band_fractions: float32 [64], replicated, may hold values from 0.02 to 0.2
- absorb_index: int32 [11, 16], replicated, may hold values from 0 to 63
- band_index: int32 [16], replicated, may hold values from 0 to 63
Outputs:
- new_state: float32 [12, 2, 32, 512], P(None, 'case', 'wall', 'azim'), parts along dimension 1
- wall_flux: float32 [2, 512], P('case', 'azim'), parts along dimension 0
The draws below stay inside these ranges and needn't reach their ends.
There are 2 independent parts, one for each index of `case`. The reference program is written for one: setup_inputs(seed, part) draws one part's arguments, and reference() takes and returns one part's arrays. A program takes and returns all parts, laid end to end along the dimension named above; an argument that names none is the same for every part. Nothing has to cross between parts.
All inputs are finite; a program needn't handle non-finite values.
Results may differ from the reference program's by a relative error of at most 0.0003.
Values sent between devices are 32-bit elements; how exact they have to be, the bound alone decides.
A program may use at most 64 MiB of HBM per device.

```python
import math
import jax
import jax.numpy as jnp
from jax import lax

STATIONS = 1
BANDS = 16
SPECIES = 11
NTAB = 64
COMPS = 12
NR = 32
NA = 512


def touch_ends(drawn, stream_key, low, largest):
    index_at = [jax.random.randint(jax.random.fold_in(stream_key, axis), (), 0, length) for axis, length in enumerate(drawn.shape)]
    main_axis = drawn.shape.index(max(drawn.shape))
    next_to = index_at[:main_axis] + [(index_at[main_axis] + 1) % drawn.shape[main_axis]] + index_at[main_axis + 1:]
    return drawn.at[tuple(index_at)].set(low).at[tuple(next_to)].set(largest)


def steps_of(stream_key, extent, pieces, least, high):
    factor_of, own = 1.0, jax.random.fold_in(stream_key, 6)
    for position, blocks in pieces:
        draws = jnp.exp(jax.random.uniform(jax.random.fold_in(own, position), (blocks,), jnp.float32, least / len(pieces), high / len(pieces)))
        factor_of = factor_of * jnp.repeat(draws, extent[position] // blocks).reshape([-1 if axis == position else 1 for axis in range(len(extent))])
    return factor_of


def setup_inputs(seed: int = 0, part: int = 0) -> dict:
    arg_keys = jax.random.split(jax.random.key(seed), 7)
    own_keys = jax.random.split(jax.random.fold_in(arg_keys[6], part), 7)
    return {
        "state": jnp.clip(0.5 + 1.0 * jax.random.uniform(own_keys[0], (COMPS, STATIONS, NR, NA), jnp.float32) ** steps_of(own_keys[0], (COMPS, STATIONS, NR, NA), ((2, 4), (3, 4)), -0.2, 0.2), 0.5, 1.5),
        "courant": jnp.clip(jax.random.uniform(own_keys[1], (STATIONS, NR, NA), jnp.float32, -0.6, 0.6) * steps_of(own_keys[1], (STATIONS, NR, NA), ((1, 4), (2, 4)), -0.4, 0.0), -0.6, 0.6),
        "cross_sections": jnp.clip(jnp.exp(jax.random.uniform(arg_keys[2], (NTAB,), jnp.float32, math.log(0.02), math.log(0.6))), 0.02, 0.6),
        "band_fractions": jnp.clip(jnp.exp(jax.random.uniform(arg_keys[3], (NTAB,), jnp.float32, math.log(0.02), math.log(0.2))), 0.02, 0.2),
        "absorb_index": touch_ends(jax.random.randint(arg_keys[4], (SPECIES, BANDS), 0, NTAB), jax.random.fold_in(arg_keys[4], 1), 0, NTAB - 1).astype(jnp.int32),
        "band_index": touch_ends(jax.random.randint(arg_keys[5], (BANDS,), 0, NTAB), jax.random.fold_in(arg_keys[5], 1), 0, NTAB - 1).astype(jnp.int32),
    }


KERNEL_WEIGHTS = (0.55, 0.45)
KERNEL_RATES = (1.15, 3.4)
FILTER_STRENGTH = 0.02
COUPLING = 0.1


def band_tables(absorb_index, band_index, cross_sections, band_fractions):
    entries = cross_sections.shape[0]
    table_slots = lax.broadcasted_iota(jnp.int32, (1, 1, entries), 2)
    spectral_absorber_area = jnp.sum(jnp.where(absorb_index[:, :, None] == table_slots, cross_sections[None, None, :], 0.0), axis=2)
    chosen_values = jnp.where(band_index[:, None] == table_slots[0], band_fractions[None, :], 0.0)
    return spectral_absorber_area, jnp.sum(chosen_values, axis=1)


def viewing_line_irradiance(kinetic_heat_level, species_concentrations, spectral_absorber_area, spectral_fraction_weight, mesh_cell_width, viewing_line_dimension):
    absorption = jnp.einsum("kb,kij->bij", spectral_absorber_area, species_concentrations, precision=lax.Precision.HIGHEST)
    optical_thickness_step = absorption * mesh_cell_width
    optical_depth = lax.cumsum(optical_thickness_step, viewing_line_dimension) - 0.5 * optical_thickness_step
    radiated_energy_rate = spectral_fraction_weight[:, None, None] * kinetic_heat_level[None] ** 4 * optical_thickness_step
    net_flux = 0.0
    wall_flux = 0.0
    for weight, decay_rate in zip(KERNEL_WEIGHTS, KERNEL_RATES):
        growth = jnp.exp(decay_rate * optical_depth)
        falloff = jnp.exp(-decay_rate * optical_depth)
        upward = falloff * lax.cumsum(radiated_energy_rate * growth, viewing_line_dimension)
        tail_sum = lax.cumsum(radiated_energy_rate * falloff, viewing_line_dimension, reverse=True)
        net_flux = net_flux + weight * jnp.sum(upward - growth * tail_sum, axis=0)
        wall_flux = wall_flux + weight * jnp.sum(lax.index_in_dim(tail_sum, 0, viewing_line_dimension, keepdims=False), axis=0)
    return net_flux, wall_flux


def edge_pad(net_flux, viewing_line_dimension):
    count = net_flux.shape[viewing_line_dimension]
    first_row = lax.slice_in_dim(net_flux, 0, 1, axis=viewing_line_dimension)
    last_row = lax.slice_in_dim(net_flux, count - 1, count, axis=viewing_line_dimension)
    return jnp.concatenate([first_row, net_flux, last_row], viewing_line_dimension)


def divergence(padded, viewing_line_dimension, mesh_cell_width):
    count = padded.shape[viewing_line_dimension] - 2
    before = lax.slice_in_dim(padded, 0, count, axis=viewing_line_dimension)
    after = lax.slice_in_dim(padded, 2, count + 2, axis=viewing_line_dimension)
    return (before - after) / (2.0 * mesh_cell_width)


def tendency(shifted, courant, heating):
    gradient = (45.0 * (shifted(1) - shifted(-1)) - 9.0 * (shifted(2) - shifted(-2)) + (shifted(3) - shifted(-3))) / 60.0
    smoothing = shifted(-3) + shifted(3) - 6.0 * (shifted(-2) + shifted(2)) + 15.0 * (shifted(-1) + shifted(1)) - 20.0 * shifted(0)
    change_sum = FILTER_STRENGTH * smoothing - courant[None] * gradient
    return change_sum.at[0].add(COUPLING * heating)


def reference(state, courant, cross_sections, band_fractions, absorb_index, band_index):
    spectral_absorber_area, spectral_fraction_weight = band_tables(absorb_index, band_index, cross_sections, band_fractions)
    mesh_cell_width = 1.0 / NR

    def segment_change(current):
        components = current.shape[0]
        line_data = jnp.transpose(current, (0, 2, 1, 3)).reshape(components, NR, STATIONS * NA)
        net_flux, wall_flux = viewing_line_irradiance(line_data[0], line_data[1:], spectral_absorber_area, spectral_fraction_weight, mesh_cell_width, 1)
        heating = divergence(edge_pad(net_flux, 0), 0, mesh_cell_width)
        heating = jnp.transpose(heating.reshape(NR, STATIONS, NA), (1, 0, 2))

        def shifted(offset):
            return jnp.roll(current, -offset, axis=3)

        return tendency(shifted, courant, heating), wall_flux.reshape(STATIONS, NA)

    first_change, first_flux = segment_change(state)
    middle = state + first_change
    second_change, second_flux = segment_change(middle)
    new_state = 0.5 * (state + middle + second_change)
    return new_state, 0.5 * (first_flux + second_flux)
```

```python
import functools

import jax
import jax.numpy as jnp
from jax import lax
from jax.experimental import pallas as pl
from jax.experimental.pallas import tpu as pltpu
from jax.sharding import PartitionSpec as P

WEIGHTS = (0.55, 0.45)
RATES = (1.15, 3.4)
FILTER = 0.02
COUPLING = 0.1
REACH = 6
MESH = pl.DeviceIdType.MESH
EXACT = lax.Precision.HIGHEST


def loop(count, body, init):
    if count <= 4:
        for i in range(count):
            init = body(i, init)
        return init
    return lax.fori_loop(0, count, body, init)


def kernel(
    walls, azims, state, courant, sections, fractions, absorb, band,
    new_state, wall_out,
    gs, gc, gl, gr, gh, ms, mh, edge_l, edge_r, em, t1, t2, net, net_h, mat,
    table, idx, cs, bf, bi,
    local_sem, s_state, r_state, s_cour, r_cour, s_left, r_left, s_right, r_right,
):
    comps, rows, lanes = state.shape
    species, bands = absorb.shape
    entries = sections.shape[0]
    total = rows * walls
    me = lax.axis_index("wall")
    az = lax.axis_index("azim")
    right, left = lax.rem(az + 1, azims), lax.rem(az + azims - 1, azims)

    def peer(d):
        return lax.rem(me + d, walls)

    def source(d):
        return lax.rem(me + walls - d, walls)

    barrier = pltpu.get_barrier_semaphore()

    def greet(d, _):
        pl.semaphore_signal(barrier, inc=1, device_id={"wall": peer(d), "azim": left}, device_id_type=MESH)
        pl.semaphore_signal(barrier, inc=1, device_id={"wall": peer(d), "azim": right}, device_id_type=MESH)
        return 0

    def greet_wall(d, _):
        pl.semaphore_signal(barrier, inc=1, device_id={"wall": peer(d + 1)}, device_id_type=MESH)
        return 0

    loop(walls - 1, greet_wall, 0)
    loop(walls, greet, 0)

    loads = [
        pltpu.make_async_copy(src, dst, local_sem.at[i])
        for i, (src, dst) in enumerate(
            [(state, gs.at[me]), (courant, gc.at[me]), (sections, cs), (fractions, bf), (absorb, idx), (band, bi)]
        )
    ]
    for c in loads:
        c.start()
    for c in loads[:2]:
        c.wait()

    lane = lax.broadcasted_iota(jnp.int32, (rows, lanes), 1)

    el = jnp.zeros((rows, lanes), jnp.float32)
    er = jnp.zeros((rows, lanes), jnp.float32)
    for c in range(comps + 1):
        x = gs[me, c] if c < comps else gc[me]
        here = (lane >= REACH * c) & (lane < REACH * (c + 1))
        el = jnp.where(here, pltpu.roll(x, REACH * c, 1) if c else x, el)
        er = jnp.where(here, pltpu.roll(x, (REACH * (c + 1)) % lanes, 1), er)
    edge_l[...] = el
    edge_r[...] = er

    pl.semaphore_wait(barrier, 3 * walls - 1)

    def state_copy(d, slot):
        return pltpu.make_async_remote_copy(
            src_ref=state, dst_ref=gs.at[slot], send_sem=s_state.at[d], recv_sem=r_state.at[d],
            device_id={"wall": peer(d)}, device_id_type=MESH)

    def cour_copy(d, slot):
        return pltpu.make_async_remote_copy(
            src_ref=courant, dst_ref=gc.at[slot], send_sem=s_cour.at[d], recv_sem=r_cour.at[d],
            device_id={"wall": peer(d)}, device_id_type=MESH)

    def left_copy(d, slot):
        return pltpu.make_async_remote_copy(
            src_ref=edge_r, dst_ref=gl.at[slot], send_sem=s_left.at[d], recv_sem=r_left.at[d],
            device_id={"wall": peer(d), "azim": right}, device_id_type=MESH)

    def right_copy(d, slot):
        return pltpu.make_async_remote_copy(
            src_ref=edge_l, dst_ref=gr.at[slot], send_sem=s_right.at[d], recv_sem=r_right.at[d],
            device_id={"wall": peer(d), "azim": left}, device_id_type=MESH)

    def send_state(i, _):
        state_copy(i + 1, me).start()
        return 0

    def send_edges(d, _):
        left_copy(d, me).start()
        right_copy(d, me).start()
        return 0

    def send_cour(i, _):
        cour_copy(i + 1, me).start()
        return 0

    loop(walls - 1, send_state, 0)
    loop(walls, send_edges, 0)
    loop(walls - 1, send_cour, 0)

    for c in loads[2:]:
        c.wait()
    index = idx[...]
    picked = lax.fori_loop(
        0, entries, lambda t, acc: jnp.where(index == t, cs[t], acc), jnp.zeros((species, bands), jnp.float32), unroll=8)
    table[...] = jnp.zeros_like(table)
    table[0:species, 0:bands] = picked
    kpad = table.shape[0]
    rb = rows * bands
    spread = jnp.where(
        lax.broadcasted_iota(jnp.int32, (rb, lanes), 0) % bands == lax.broadcasted_iota(jnp.int32, (rb, lanes), 1), 1.0, 0.0)
    by_row = lax.dot_general(spread, table[...], (((1,), (1,)), ((), ())), precision=EXACT, preferred_element_type=jnp.float32)
    cr = comps * rows
    columns = jnp.where(
        lax.broadcasted_iota(jnp.int32, (kpad, cr), 1) // rows == lax.broadcasted_iota(jnp.int32, (kpad, cr), 0) + 1, 1.0, 0.0)
    full = jnp.dot(by_row, columns, precision=EXACT, preferred_element_type=jnp.float32)
    same_row = lax.broadcasted_iota(jnp.int32, (rb, cr), 0) // bands == lax.broadcasted_iota(jnp.int32, (rb, cr), 1) % rows
    mat[...] = jnp.where(same_row, full, 0.0) * (1.0 / total)
    band_row = lax.broadcasted_iota(jnp.int32, (bands, lanes), 0)
    share = jnp.zeros((bands, lanes), jnp.float32)
    for b in range(bands):
        share = jnp.where(band_row == b, bf[bi[b]], share)
    diff_r = lax.broadcasted_iota(jnp.int32, (rows, (rows + 2) * 8), 1) // 8
    diff_i = lax.broadcasted_iota(jnp.int32, (rows, (rows + 2) * 8), 0)
    diff = jnp.where(diff_r == diff_i, 1.0, 0.0) - jnp.where(diff_r == diff_i + 2, 1.0, 0.0)
    heat_scale = COUPLING * total / 2.0

    def cells(ref, z):
        u = ref[z][0:comps].reshape(cr, lanes)
        step = jnp.dot(mat[...], u, precision=EXACT, preferred_element_type=jnp.float32)
        t = ref[z, 0]
        t = t * t
        t = t * t
        t1[z] = jnp.exp(step * (-0.5 * RATES[0]))
        t2[z] = jnp.exp(step * (-0.5 * RATES[1]))
        for r in range(rows):
            part = slice(r * bands, (r + 1) * bands)
            em[z, part] = step[part] * (share * t[r : r + 1])

    def scan(out):
        zero = jnp.zeros((bands, lanes), jnp.float32)

        def fold(a):
            s = a[0:8]
            for k in range(8, bands, 8):
                s = s + a[k : k + 8]
            return s

        def up(z, carry):
            u1, u2, a1, a2 = carry
            for r in range(rows):
                part = slice(r * bands, (r + 1) * bands)
                e, b1, b2 = em[z, part], t1[z, part], t2[z, part]
                u1 = WEIGHTS[0] * e + (a1 * b1) * u1
                u2 = WEIGHTS[1] * e + (a2 * b2) * u2
                out[1 + z * rows + r] = fold(u1 + u2)
                a1, a2 = b1, b2
            return u1, u2, a1, a2

        def down(i, carry):
            d1, d2, a1, a2 = carry
            z = walls - 1 - i
            for r in reversed(range(rows)):
                part = slice(r * bands, (r + 1) * bands)
                e, b1, b2 = em[z, part], t1[z, part], t2[z, part]
                d1 = WEIGHTS[0] * e + (a1 * b1) * d1
                d2 = WEIGHTS[1] * e + (a2 * b2) * d2
                at = 1 + z * rows + r
                out[at] = out[at] - fold(d1 + d2)
                a1, a2 = b1, b2
            return d1, d2, a1, a2

        loop(walls, up, (zero, zero, zero, zero))
        d1, d2, a1, a2 = loop(walls, down, (zero, zero, zero, zero))
        out[0] = out[1]
        out[total + 1] = out[total]
        return jnp.sum(fold(a1 * d1 + a2 * d2), axis=0, keepdims=True)

    def heat(ref, z):
        part = ref[pl.ds(z * rows, rows + 2)].reshape((rows + 2) * 8, lanes)
        return heat_scale * jnp.dot(diff, part, precision=EXACT, preferred_element_type=jnp.float32)

    def shifts(x, h):
        own, halo = {0: x}, {0: h}
        for o in (1, 2, 3, -1, -2, -3):
            rx, rh = pltpu.roll(x, (-o) % lanes, 1), pltpu.roll(h, (-o) % lanes, 1)
            inside = lane < lanes - o if o > 0 else lane >= -o
            own[o] = jnp.where(inside, rx, rh)
            halo[o] = jnp.where(inside, rh, rx)
        return own, halo

    def tendency(s, cour):
        gradient = (45.0 / 60.0) * (s[1] - s[-1]) - (9.0 / 60.0) * (s[2] - s[-2]) + (1.0 / 60.0) * (s[3] - s[-3])
        smooth = (s[-3] + s[3]) - 6.0 * (s[-2] + s[2]) + 15.0 * (s[-1] + s[1]) - 20.0 * s[0]
        return FILTER * smooth - cour * gradient

    def arrive(d, _):
        if isinstance(d, int) and d == 0:
            cells(gs, me)
            return 0
        state_copy(d, source(d)).wait_recv()
        cells(gs, source(d))
        return 0

    cells(gs, me)
    loop(walls - 1, lambda i, _: arrive(i + 1, _), 0)
    flux = scan(net)

    def halos(d, _):
        left_copy(d, source(d)).wait_recv()
        right_copy(d, source(d)).wait_recv()
        z = source(d)
        pr, pk = gr[z], gl[z]
        for c in range(comps + 1):
            a = pltpu.roll(pr, lanes - REACH * c, 1) if c else pr
            b = pltpu.roll(pk, lanes - REACH * (c + 1), 1)
            gh[z, c] = jnp.where(lane < lanes // 2, a, b)
        cells(gh, z)
        return 0

    loop(walls, halos, 0)
    scan(net_h)

    def wait_cour(i, _):
        cour_copy(i + 1, source(i + 1)).wait_recv()
        return 0

    loop(walls - 1, wait_cour, 0)

    def middle(z, _):
        cour = gc[z]
        for c in range(comps):
            x = gs[z, c]
            own, _h = shifts(x, gh[z, c])
            change = tendency(own, cour)
            if c == 0:
                change = change + heat(net, z)
            ms[z, c] = x + change
        cells(ms, z)
        return 0

    loop(walls, middle, 0)
    flux = flux + scan(net)
    wall_out[...] = 0.5 * flux
    hc = gh[me, comps]
    for c in range(comps):
        h = gh[me, c]
        _o, halo = shifts(gs[me, c], h)
        change = tendency(halo, hc)
        if c == 0:
            change = change + heat(net_h, me)
        mh[c] = h + change

    cour = gc[me]
    for c in range(comps):
        x = ms[me, c]
        own, _h = shifts(x, mh[c])
        change = tendency(own, cour)
        if c == 0:
            change = change + heat(net, me)
        new_state[c] = 0.5 * (gs[me, c] + x + change)

    def finish_wall(i, _):
        state_copy(i + 1, me).wait_send()
        cour_copy(i + 1, me).wait_send()
        return 0

    def finish_edges(d, _):
        left_copy(d, me).wait_send()
        right_copy(d, me).wait_send()
        return 0

    loop(walls - 1, finish_wall, 0)
    loop(walls, finish_edges, 0)


def local(walls, azims, state, courant, cross_sections, band_fractions, absorb_index, band_index):
    comps, stations, rows, lanes = state.shape
    bands = absorb_index.shape[1]
    species = absorb_index.shape[0]
    entries = cross_sections.shape[0]
    total = rows * walls
    f32 = jnp.float32
    vmem = pltpu.VMEM
    dma = pltpu.SemaphoreType.DMA
    any_spec = pl.BlockSpec(memory_space=pl.ANY)
    vmem_spec = pl.BlockSpec(memory_space=pltpu.VMEM)
    new_state, wall = pl.pallas_call(
        functools.partial(kernel, walls, azims),
        out_shape=(
            jax.ShapeDtypeStruct((comps, rows, lanes), f32),
            jax.ShapeDtypeStruct((1, lanes), f32),
        ),
        in_specs=[any_spec] * 6,
        out_specs=(vmem_spec, vmem_spec),
        scratch_shapes=[
            vmem((walls, comps, rows, lanes), f32),
            vmem((walls, rows, lanes), f32),
            vmem((walls, rows, lanes), f32),
            vmem((walls, rows, lanes), f32),
            vmem((walls, comps + 1, rows, lanes), f32),
            vmem((walls, comps, rows, lanes), f32),
            vmem((comps, rows, lanes), f32),
            vmem((rows, lanes), f32),
            vmem((rows, lanes), f32),
            vmem((walls, rows * bands, lanes), f32),
            vmem((walls, rows * bands, lanes), f32),
            vmem((walls, rows * bands, lanes), f32),
            vmem((total + 2, 8, lanes), f32),
            vmem((total + 2, 8, lanes), f32),
            vmem((rows * bands, comps * rows), f32),
            vmem((16, lanes), f32),
            vmem((species, bands), jnp.int32),
            pltpu.SMEM((entries,), f32),
            pltpu.SMEM((entries,), f32),
            pltpu.SMEM((bands,), jnp.int32),
            dma((6,)),
        ] + [dma((walls,))] * 8,
        compiler_params=pltpu.CompilerParams(
            collective_id=0, has_side_effects=True, vmem_limit_bytes=48 * 1024 * 1024),
    )(state.reshape(comps, rows, lanes), courant.reshape(rows, lanes), cross_sections, band_fractions, absorb_index, band_index)
    return new_state.reshape(state.shape), wall


def solution(mesh):
    return jax.shard_map(
        functools.partial(local, mesh.shape["wall"], mesh.shape["azim"]),
        mesh=mesh,
        in_specs=(P(None, "case", "wall", "azim"), P("case", "wall", "azim"), P(), P(), P(), P()),
        out_specs=(P(None, "case", "wall", "azim"), P("case", "azim")),
        check_vma=False,
    )
```

```python
import functools

import jax
import jax.numpy as jnp
from jax import lax
from jax.experimental import pallas as pl
from jax.experimental.pallas import tpu as pltpu
from jax.sharding import PartitionSpec as P

WEIGHTS = (0.55, 0.45)
RATES = (1.15, 3.4)
FILTER = 0.02
COUPLING = 0.1
REACH = 6
MESH = pl.DeviceIdType.MESH
EXACT = lax.Precision.HIGHEST


def loop(count, body, init):
    if count <= 4:
        for i in range(count):
            init = body(i, init)
        return init
    return lax.fori_loop(0, count, body, init)


def kernel(
    walls, azims, state, courant, sections, fractions, absorb, band,
    new_state, wall_out,
    gs, gc, gl, gr, gh, ms, mh, edge_l, edge_r, em, t1, t2, net, net_h, mat,
    table, idx, cs, bf, bi,
    local_sem, edge_sem, s_state, r_state, s_cour, r_cour,
):
    comps, rows, lanes = state.shape
    species, bands = absorb.shape
    entries = sections.shape[0]
    total = rows * walls
    me = lax.axis_index("wall")
    az = lax.axis_index("azim")
    right, left = lax.rem(az + 1, azims), lax.rem(az + azims - 1, azims)

    def peer(d):
        return lax.rem(me + d, walls)

    def source(d):
        return lax.rem(me + walls - d, walls)

    barrier = pltpu.get_barrier_semaphore()

    def greet(i, _):
        pl.semaphore_signal(barrier, inc=1, device_id={"wall": peer(i + 1)}, device_id_type=MESH)
        return 0

    loop(walls - 1, greet, 0)
    for side in (left, right):
        pl.semaphore_signal(barrier, inc=1, device_id={"azim": side}, device_id_type=MESH)

    loads = [
        pltpu.make_async_copy(src, dst, local_sem.at[i])
        for i, (src, dst) in enumerate(
            [(state, gs.at[me]), (courant, gc.at[me, 0]), (sections, cs), (fractions, bf), (absorb, idx), (band, bi)]
        )
    ]
    for c in loads:
        c.start()
    lane = lax.broadcasted_iota(jnp.int32, (rows, lanes), 1)

    pl.semaphore_wait(barrier, walls + 1)

    def state_copy(d, slot):
        return pltpu.make_async_remote_copy(
            src_ref=state, dst_ref=gs.at[slot], send_sem=s_state.at[d], recv_sem=r_state.at[d],
            device_id={"wall": peer(d)}, device_id_type=MESH)

    def line_copy(d, slot):
        return pltpu.make_async_remote_copy(
            src_ref=gc.at[me], dst_ref=gc.at[slot], send_sem=s_cour.at[d], recv_sem=r_cour.at[d],
            device_id={"wall": peer(d)}, device_id_type=MESH)

    def send_state(i, _):
        state_copy(i + 1, me).start()
        return 0

    def send_line(i, _):
        line_copy(i + 1, me).start()
        return 0

    loop(walls - 1, send_state, 0)

    for c in loads[:2]:
        c.wait()
    el = jnp.zeros((rows, lanes), jnp.float32)
    er = jnp.zeros((rows, lanes), jnp.float32)
    for c in range(comps + 1):
        x = gs[me, c] if c < comps else gc[me, 0]
        here = (lane >= REACH * c) & (lane < REACH * (c + 1))
        el = jnp.where(here, pltpu.roll(x, REACH * c, 1) if c else x, el)
        er = jnp.where(here, pltpu.roll(x, (REACH * (c + 1)) % lanes, 1), er)
    edge_l[...] = el
    edge_r[...] = er

    edges = [
        pltpu.make_async_remote_copy(
            src_ref=src, dst_ref=dst, send_sem=edge_sem.at[2 * i], recv_sem=edge_sem.at[2 * i + 1],
            device_id={"azim": to}, device_id_type=MESH)
        for i, (src, dst, to) in enumerate([(edge_r, gl, right), (edge_l, gr, left)])
    ]
    for c in edges:
        c.start()

    for c in loads[2:]:
        c.wait()
    index = idx[...]
    picked = lax.fori_loop(
        0, entries, lambda t, acc: jnp.where(index == t, cs[t], acc), jnp.zeros((species, bands), jnp.float32), unroll=8)
    table[...] = jnp.zeros_like(table)
    table[0:species, 0:bands] = picked
    kpad = table.shape[0]
    rb = rows * bands
    spread = jnp.where(
        lax.broadcasted_iota(jnp.int32, (rb, lanes), 0) & (bands - 1) == lax.broadcasted_iota(jnp.int32, (rb, lanes), 1), 1.0, 0.0)
    by_row = lax.dot_general(spread, table[...], (((1,), (1,)), ((), ())), precision=EXACT, preferred_element_type=jnp.float32)
    cr = comps * rows
    columns = jnp.where(
        lax.broadcasted_iota(jnp.int32, (kpad, cr), 1) // rows == lax.broadcasted_iota(jnp.int32, (kpad, cr), 0) + 1, 1.0, 0.0)
    full = jnp.dot(by_row, columns, precision=EXACT, preferred_element_type=jnp.float32)
    same_row = lax.broadcasted_iota(jnp.int32, (rb, cr), 0) // bands == lax.broadcasted_iota(jnp.int32, (rb, cr), 1) % rows
    mat[...] = jnp.where(same_row, full, 0.0) * (1.0 / total)
    band_row = lax.broadcasted_iota(jnp.int32, (bands, lanes), 0)
    share = jnp.zeros((bands, lanes), jnp.float32)
    for b in range(bands):
        share = jnp.where(band_row == b, bf[bi[b]], share)
    diff_r = lax.broadcasted_iota(jnp.int32, (rows, (rows + 2) * 8), 1) // 8
    diff_i = lax.broadcasted_iota(jnp.int32, (rows, (rows + 2) * 8), 0)
    diff = jnp.where(diff_r == diff_i, 1.0, 0.0) - jnp.where(diff_r == diff_i + 2, 1.0, 0.0)
    heat_scale = COUPLING * total / 2.0

    def cells(ref, z):
        u = ref[z][0:comps].reshape(cr, lanes)
        step = jnp.dot(mat[...], u, precision=EXACT, preferred_element_type=jnp.float32)
        t = ref[z, 0]
        t = t * t
        t = t * t
        t1[z] = jnp.exp(step * (-0.5 * RATES[0]))
        t2[z] = jnp.exp(step * (-0.5 * RATES[1]))
        for r in range(rows):
            part = slice(r * bands, (r + 1) * bands)
            em[z, part] = step[part] * (share * t[r : r + 1])

    def scan(out):
        zero = jnp.zeros((bands, lanes), jnp.float32)

        def fold(a):
            s = a[0:8]
            for k in range(8, bands, 8):
                s = s + a[k : k + 8]
            return s

        def up(z, carry):
            u1, u2, a1, a2 = carry
            for r in range(rows):
                part = slice(r * bands, (r + 1) * bands)
                e, b1, b2 = em[z, part], t1[z, part], t2[z, part]
                u1 = WEIGHTS[0] * e + (a1 * b1) * u1
                u2 = WEIGHTS[1] * e + (a2 * b2) * u2
                out[1 + z * rows + r] = fold(u1 + u2)
                a1, a2 = b1, b2
            return u1, u2, a1, a2

        def down(i, carry):
            d1, d2, a1, a2 = carry
            z = walls - 1 - i
            for r in reversed(range(rows)):
                part = slice(r * bands, (r + 1) * bands)
                e, b1, b2 = em[z, part], t1[z, part], t2[z, part]
                d1 = WEIGHTS[0] * e + (a1 * b1) * d1
                d2 = WEIGHTS[1] * e + (a2 * b2) * d2
                at = 1 + z * rows + r
                out[at] = out[at] - fold(d1 + d2)
                a1, a2 = b1, b2
            return d1, d2, a1, a2

        loop(walls, up, (zero, zero, zero, zero))
        d1, d2, a1, a2 = loop(walls, down, (zero, zero, zero, zero))
        out[0] = out[1]
        out[total + 1] = out[total]
        return jnp.sum(fold(a1 * d1 + a2 * d2), axis=0, keepdims=True)

    def heat(ref, z):
        part = ref[pl.ds(z * rows, rows + 2)].reshape((rows + 2) * 8, lanes)
        return heat_scale * jnp.dot(diff, part, precision=EXACT, preferred_element_type=jnp.float32)

    def shifts(x, h):
        own, halo = {0: x}, {0: h}
        for o in (1, 2, 3, -1, -2, -3):
            rx, rh = pltpu.roll(x, (-o) % lanes, 1), pltpu.roll(h, (-o) % lanes, 1)
            inside = lane < lanes - o if o > 0 else lane >= -o
            own[o] = jnp.where(inside, rx, rh)
            halo[o] = jnp.where(inside, rh, rx)
        return own, halo

    def tendency(s, cour):
        gradient = (45.0 / 60.0) * (s[1] - s[-1]) - (9.0 / 60.0) * (s[2] - s[-2]) + (1.0 / 60.0) * (s[3] - s[-3])
        smooth = (s[-3] + s[3]) - 6.0 * (s[-2] + s[2]) + 15.0 * (s[-1] + s[1]) - 20.0 * s[0]
        return FILTER * smooth - cour * gradient

    def unpack(z, pr, pk):
        for c in range(comps + 1):
            a = pltpu.roll(pr, lanes - REACH * c, 1) if c else pr
            b = pltpu.roll(pk, lanes - REACH * (c + 1), 1)
            gh[z, c] = jnp.where(lane < lanes // 2, a, b)
        cells(gh, z)

    cells(gs, me)
    for c in edges:
        c.wait_recv()
    gc[me, 1] = jnp.where(lane % REACH < REACH // 2, gr[...], gl[...])
    loop(walls - 1, send_line, 0)

    def arrive(i, _):
        z = source(i + 1)
        state_copy(i + 1, z).wait_recv()
        cells(gs, z)
        return 0

    loop(walls - 1, arrive, 0)
    flux = scan(net)
    unpack(me, gr[...], gl[...])

    def halos(i, _):
        z = source(i + 1)
        line_copy(i + 1, z).wait_recv()
        packed = gc[z, 1]
        unpack(z, packed, packed)
        return 0

    loop(walls - 1, halos, 0)
    scan(net_h)

    def middle(z, _):
        cour = gc[z, 0]
        for c in range(comps):
            x = gs[z, c]
            own, _h = shifts(x, gh[z, c])
            change = tendency(own, cour)
            if c == 0:
                change = change + heat(net, z)
            ms[z, c] = x + change
        cells(ms, z)
        return 0

    loop(walls, middle, 0)
    flux = flux + scan(net)
    wall_out[...] = 0.5 * flux
    hc = gh[me, comps]
    for c in range(comps):
        h = gh[me, c]
        _o, halo = shifts(gs[me, c], h)
        change = tendency(halo, hc)
        if c == 0:
            change = change + heat(net_h, me)
        mh[c] = h + change

    cour = gc[me, 0]
    for c in range(comps):
        x = ms[me, c]
        own, _h = shifts(x, mh[c])
        change = tendency(own, cour)
        if c == 0:
            change = change + heat(net, me)
        new_state[c] = 0.5 * (gs[me, c] + x + change)

    def finish(i, _):
        state_copy(i + 1, me).wait_send()
        line_copy(i + 1, me).wait_send()
        return 0

    loop(walls - 1, finish, 0)
    for c in edges:
        c.wait_send()


def local(walls, azims, state, courant, cross_sections, band_fractions, absorb_index, band_index):
    comps, stations, rows, lanes = state.shape
    bands = absorb_index.shape[1]
    species = absorb_index.shape[0]
    entries = cross_sections.shape[0]
    total = rows * walls
    f32 = jnp.float32
    vmem = pltpu.VMEM
    dma = pltpu.SemaphoreType.DMA
    hbm_spec = pl.BlockSpec(memory_space=pltpu.HBM)
    vmem_spec = pl.BlockSpec(memory_space=pltpu.VMEM)
    new_state, wall = pl.pallas_call(
        functools.partial(kernel, walls, azims),
        out_shape=(
            jax.ShapeDtypeStruct((comps, rows, lanes), f32),
            jax.ShapeDtypeStruct((1, lanes), f32),
        ),
        in_specs=[hbm_spec] * 6,
        out_specs=(vmem_spec, vmem_spec),
        scratch_shapes=[
            vmem((walls, comps, rows, lanes), f32),
            vmem((walls, 2, rows, lanes), f32),
            vmem((rows, lanes), f32),
            vmem((rows, lanes), f32),
            vmem((walls, comps + 1, rows, lanes), f32),
            vmem((walls, comps, rows, lanes), f32),
            vmem((comps, rows, lanes), f32),
            vmem((rows, lanes), f32),
            vmem((rows, lanes), f32),
            vmem((walls, rows * bands, lanes), f32),
            vmem((walls, rows * bands, lanes), f32),
            vmem((walls, rows * bands, lanes), f32),
            vmem((total + 2, 8, lanes), f32),
            vmem((total + 2, 8, lanes), f32),
            vmem((rows * bands, comps * rows), f32),
            vmem((16, lanes), f32),
            vmem((species, bands), jnp.int32),
            pltpu.SMEM((entries,), f32),
            pltpu.SMEM((entries,), f32),
            pltpu.SMEM((bands,), jnp.int32),
            dma((6,)),
            dma((4,)),
        ] + [dma((walls,))] * 4,
        compiler_params=pltpu.CompilerParams(
            collective_id=0, has_side_effects=True, vmem_limit_bytes=58 * 1024 * 1024),
    )(state.reshape(comps, rows, lanes), courant.reshape(rows, lanes), cross_sections, band_fractions, absorb_index, band_index)
    return new_state.reshape(state.shape), wall


def solution(mesh):
    return jax.shard_map(
        functools.partial(local, mesh.shape["wall"], mesh.shape["azim"]),
        mesh=mesh,
        in_specs=(P(None, "case", "wall", "azim"), P("case", "wall", "azim"), P(), P(), P(), P()),
        out_specs=(P(None, "case", "wall", "azim"), P("case", "azim")),
        check_vma=False,
    )
```

```python
import functools

import jax
import jax.numpy as jnp
from jax import lax
from jax.experimental import pallas as pl
from jax.experimental.pallas import tpu as pltpu
from jax.sharding import PartitionSpec as P

WEIGHTS = (0.55, 0.45)
RATES = (1.15, 3.4)
FILTER = 0.02
COUPLING = 0.1
REACH = 6
MESH = pl.DeviceIdType.MESH
EXACT = lax.Precision.HIGHEST


def loop(count, body, init):
    if count <= 4:
        for i in range(count):
            init = body(i, init)
        return init
    return lax.fori_loop(0, count, body, init)


def kernel(
    walls, azims, state, courant, sections, fractions, absorb, band,
    new_state, wall_out,
    gs, gc, gl, gr, gh, ms, mh, edge_l, edge_r, em, t1, t2, net, net_h, mat,
    table, idx, cs, bf, bi,
    local_sem, edge_sem, s_state, r_state, s_cour, r_cour,
):
    comps, rows, lanes = state.shape
    species, bands = absorb.shape
    entries = sections.shape[0]
    total = rows * walls
    me = lax.axis_index("wall")
    az = lax.axis_index("azim")
    right, left = lax.rem(az + 1, azims), lax.rem(az + azims - 1, azims)

    def peer(d):
        return lax.rem(me + d, walls)

    def source(d):
        return lax.rem(me + walls - d, walls)

    barrier = pltpu.get_barrier_semaphore()

    def greet(i, _):
        pl.semaphore_signal(barrier, inc=1, device_id={"wall": peer(i + 1)}, device_id_type=MESH)
        return 0

    loop(walls - 1, greet, 0)
    for side in (left, right):
        pl.semaphore_signal(barrier, inc=1, device_id={"azim": side}, device_id_type=MESH)

    loads = [
        pltpu.make_async_copy(src, dst, local_sem.at[i])
        for i, (src, dst) in enumerate(
            [(state, gs.at[me]), (courant, gc.at[me, 0]), (sections, cs), (fractions, bf), (absorb, idx), (band, bi)]
        )
    ]
    for c in loads:
        c.start()
    lane = lax.broadcasted_iota(jnp.int32, (rows, lanes), 1)

    pl.semaphore_wait(barrier, walls + 1)

    def state_copy(d, slot):
        return pltpu.make_async_remote_copy(
            src_ref=state, dst_ref=gs.at[slot], send_sem=s_state.at[d], recv_sem=r_state.at[d],
            device_id={"wall": peer(d)}, device_id_type=MESH)

    def line_copy(d, slot):
        return pltpu.make_async_remote_copy(
            src_ref=gc.at[me], dst_ref=gc.at[slot], send_sem=s_cour.at[d], recv_sem=r_cour.at[d],
            device_id={"wall": peer(d)}, device_id_type=MESH)

    def send_state(i, _):
        state_copy(i + 1, me).start()
        return 0

    def send_line(i, _):
        line_copy(i + 1, me).start()
        return 0

    loop(walls - 1, send_state, 0)

    for c in loads[:2]:
        c.wait()
    el = jnp.zeros((rows, lanes), jnp.float32)
    er = jnp.zeros((rows, lanes), jnp.float32)
    for c in range(comps + 1):
        x = gs[me, c] if c < comps else gc[me, 0]
        here = (lane >= REACH * c) & (lane < REACH * (c + 1))
        el = jnp.where(here, pltpu.roll(x, REACH * c, 1) if c else x, el)
        er = jnp.where(here, pltpu.roll(x, (REACH * (c + 1)) % lanes, 1), er)
    edge_l[...] = el
    edge_r[...] = er

    edges = [
        pltpu.make_async_remote_copy(
            src_ref=src, dst_ref=dst, send_sem=edge_sem.at[2 * i], recv_sem=edge_sem.at[2 * i + 1],
            device_id={"azim": to}, device_id_type=MESH)
        for i, (src, dst, to) in enumerate([(edge_r, gl, right), (edge_l, gr, left)])
    ]
    for c in edges:
        c.start()

    for c in loads[2:]:
        c.wait()
    index = idx[...]
    picked = lax.fori_loop(
        0, entries, lambda t, acc: jnp.where(index == t, cs[t], acc), jnp.zeros((species, bands), jnp.float32), unroll=8)
    table[...] = jnp.zeros_like(table)
    table[0:species, 0:bands] = picked
    kpad = table.shape[0]
    rb = rows * bands
    spread = jnp.where(
        lax.broadcasted_iota(jnp.int32, (rb, lanes), 0) & (bands - 1) == lax.broadcasted_iota(jnp.int32, (rb, lanes), 1), 1.0, 0.0)
    by_row = lax.dot_general(spread, table[...], (((1,), (1,)), ((), ())), precision=EXACT, preferred_element_type=jnp.float32)
    cr = comps * rows
    columns = jnp.where(
        lax.broadcasted_iota(jnp.int32, (kpad, cr), 1) // rows == lax.broadcasted_iota(jnp.int32, (kpad, cr), 0) + 1, 1.0, 0.0)
    full = jnp.dot(by_row, columns, precision=EXACT, preferred_element_type=jnp.float32)
    same_row = lax.broadcasted_iota(jnp.int32, (rb, cr), 0) // bands == lax.broadcasted_iota(jnp.int32, (rb, cr), 1) % rows
    mat[...] = jnp.where(same_row, full, 0.0) * (1.0 / total)
    band_row = lax.broadcasted_iota(jnp.int32, (bands, lanes), 0)
    share = jnp.zeros((bands, lanes), jnp.float32)
    for b in range(bands):
        share = jnp.where(band_row == b, bf[bi[b]], share)
    diff_r = lax.broadcasted_iota(jnp.int32, (rows, (rows + 2) * 8), 1) // 8
    diff_i = lax.broadcasted_iota(jnp.int32, (rows, (rows + 2) * 8), 0)
    diff = jnp.where(diff_r == diff_i, 1.0, 0.0) - jnp.where(diff_r == diff_i + 2, 1.0, 0.0)
    heat_scale = COUPLING * total / 2.0

    def cells(ref, z):
        u = ref[z][0:comps].reshape(cr, lanes)
        step = jnp.dot(mat[...], u, precision=EXACT, preferred_element_type=jnp.float32)
        t = ref[z, 0]
        t = t * t
        t = t * t
        t1[z] = jnp.exp(step * (-0.5 * RATES[0]))
        t2[z] = jnp.exp(step * (-0.5 * RATES[1]))
        for r in range(rows):
            part = slice(r * bands, (r + 1) * bands)
            em[z, part] = step[part] * (share * t[r : r + 1])

    def scan(out):
        zero = jnp.zeros((bands, lanes), jnp.float32)

        def fold(a):
            s = a[0:8]
            for k in range(8, bands, 8):
                s = s + a[k : k + 8]
            return s

        def up(z, carry):
            u1, u2, a1, a2 = carry
            for r in range(rows):
                part = slice(r * bands, (r + 1) * bands)
                e, b1, b2 = em[z, part], t1[z, part], t2[z, part]
                u1 = WEIGHTS[0] * e + (a1 * b1) * u1
                u2 = WEIGHTS[1] * e + (a2 * b2) * u2
                out[1 + z * rows + r] = fold(u1 + u2)
                a1, a2 = b1, b2
            return u1, u2, a1, a2

        def down(i, carry):
            d1, d2, a1, a2 = carry
            z = walls - 1 - i
            for r in reversed(range(rows)):
                part = slice(r * bands, (r + 1) * bands)
                e, b1, b2 = em[z, part], t1[z, part], t2[z, part]
                d1 = WEIGHTS[0] * e + (a1 * b1) * d1
                d2 = WEIGHTS[1] * e + (a2 * b2) * d2
                at = 1 + z * rows + r
                out[at] = out[at] - fold(d1 + d2)
                a1, a2 = b1, b2
            return d1, d2, a1, a2

        loop(walls, up, (zero, zero, zero, zero))
        d1, d2, a1, a2 = loop(walls, down, (zero, zero, zero, zero))
        out[0] = out[1]
        out[total + 1] = out[total]
        return jnp.sum(fold(a1 * d1 + a2 * d2), axis=0, keepdims=True)

    def heat(ref, z):
        part = ref[pl.ds(z * rows, rows + 2)].reshape((rows + 2) * 8, lanes)
        return heat_scale * jnp.dot(diff, part, precision=EXACT, preferred_element_type=jnp.float32)

    def shifts(x, h):
        own, halo = {0: x}, {0: h}
        for o in (1, 2, 3, -1, -2, -3):
            rx, rh = pltpu.roll(x, (-o) % lanes, 1), pltpu.roll(h, (-o) % lanes, 1)
            inside = lane < lanes - o if o > 0 else lane >= -o
            own[o] = jnp.where(inside, rx, rh)
            halo[o] = jnp.where(inside, rh, rx)
        return own, halo

    def tendency(s, cour):
        gradient = (45.0 / 60.0) * (s[1] - s[-1]) - (9.0 / 60.0) * (s[2] - s[-2]) + (1.0 / 60.0) * (s[3] - s[-3])
        smooth = (s[-3] + s[3]) - 6.0 * (s[-2] + s[2]) + 15.0 * (s[-1] + s[1]) - 20.0 * s[0]
        return FILTER * smooth - cour * gradient

    def unpack(z, pr, pk):
        for c in range(comps + 1):
            a = pltpu.roll(pr, lanes - REACH * c, 1) if c else pr
            b = pltpu.roll(pk, lanes - REACH * (c + 1), 1)
            gh[z, c] = jnp.where(lane < lanes // 2, a, b)
        cells(gh, z)

    cells(gs, me)
    for c in edges:
        c.wait_recv()
    gc[me, 1] = jnp.where(lane % REACH < REACH // 2, gr[...], gl[...])
    loop(walls - 1, send_line, 0)

    def arrive(i, _):
        z = source(i + 1)
        state_copy(i + 1, z).wait_recv()
        cells(gs, z)
        return 0

    loop(walls - 1, arrive, 0)
    flux = scan(net)
    unpack(me, gr[...], gl[...])

    def halos(i, _):
        z = source(i + 1)
        line_copy(i + 1, z).wait_recv()
        packed = gc[z, 1]
        unpack(z, packed, packed)
        return 0

    loop(walls - 1, halos, 0)
    scan(net_h)

    def middle(z, _):
        cour = gc[z, 0]
        for c in range(comps):
            x = gs[z, c]
            own, _h = shifts(x, gh[z, c])
            change = tendency(own, cour)
            if c == 0:
                change = change + heat(net, z)
            ms[z, c] = x + change
        cells(ms, z)
        return 0

    loop(walls, middle, 0)
    flux = flux + scan(net)
    wall_out[...] = 0.5 * flux
    hc = gh[me, comps]
    for c in range(comps):
        h = gh[me, c]
        _o, halo = shifts(gs[me, c], h)
        change = tendency(halo, hc)
        if c == 0:
            change = change + heat(net_h, me)
        mh[c] = h + change

    cour = gc[me, 0]
    for c in range(comps):
        x = ms[me, c]
        own, _h = shifts(x, mh[c])
        change = tendency(own, cour)
        if c == 0:
            change = change + heat(net, me)
        new_state[c] = 0.5 * (gs[me, c] + x + change)

    def finish(i, _):
        state_copy(i + 1, me).wait_send()
        line_copy(i + 1, me).wait_send()
        return 0

    loop(walls - 1, finish, 0)
    for c in edges:
        c.wait_send()


def hand_over(a, b, a_out, b_out, sems):
    copies = [pltpu.make_async_copy(a, a_out, sems.at[0]), pltpu.make_async_copy(b, b_out, sems.at[1])]
    for c in copies:
        c.start()
    for c in copies:
        c.wait()


def local(walls, azims, state, courant, cross_sections, band_fractions, absorb_index, band_index):
    comps, stations, rows, lanes = state.shape
    bands = absorb_index.shape[1]
    species = absorb_index.shape[0]
    entries = cross_sections.shape[0]
    total = rows * walls
    f32 = jnp.float32
    vmem = pltpu.VMEM
    dma = pltpu.SemaphoreType.DMA
    hbm_spec = pl.BlockSpec(memory_space=pltpu.HBM)
    vmem_spec = pl.BlockSpec(memory_space=pltpu.VMEM)
    new_state, wall = pl.pallas_call(
        functools.partial(kernel, walls, azims),
        out_shape=(
            pltpu.VMEM((comps, rows, lanes), f32),
            pltpu.VMEM((1, lanes), f32),
        ),
        in_specs=[hbm_spec] * 6,
        out_specs=(vmem_spec, vmem_spec),
        scratch_shapes=[
            vmem((walls, comps, rows, lanes), f32),
            vmem((walls, 2, rows, lanes), f32),
            vmem((rows, lanes), f32),
            vmem((rows, lanes), f32),
            vmem((walls, comps + 1, rows, lanes), f32),
            vmem((walls, comps, rows, lanes), f32),
            vmem((comps, rows, lanes), f32),
            vmem((rows, lanes), f32),
            vmem((rows, lanes), f32),
            vmem((walls, rows * bands, lanes), f32),
            vmem((walls, rows * bands, lanes), f32),
            vmem((walls, rows * bands, lanes), f32),
            vmem((total + 2, 8, lanes), f32),
            vmem((total + 2, 8, lanes), f32),
            vmem((rows * bands, comps * rows), f32),
            vmem((16, lanes), f32),
            vmem((species, bands), jnp.int32),
            pltpu.SMEM((entries,), f32),
            pltpu.SMEM((entries,), f32),
            pltpu.SMEM((bands,), jnp.int32),
            dma((6,)),
            dma((4,)),
        ] + [dma((walls,))] * 4,
        compiler_params=pltpu.CompilerParams(
            collective_id=0, has_side_effects=True, vmem_limit_bytes=58 * 1024 * 1024),
    )(state.reshape(comps, rows, lanes), courant.reshape(rows, lanes), cross_sections, band_fractions, absorb_index, band_index)
    hbm = pl.BlockSpec(memory_space=pltpu.HBM)
    new_state, wall = pl.pallas_call(
        hand_over,
        out_shape=(
            jax.ShapeDtypeStruct((comps, rows, lanes), f32),
            jax.ShapeDtypeStruct((1, lanes), f32),
        ),
        in_specs=[pl.BlockSpec(memory_space=pl.ANY)] * 2,
        out_specs=(hbm, hbm),
        scratch_shapes=[dma((2,))],
    )(pltpu.with_memory_space_constraint(new_state, pltpu.VMEM), pltpu.with_memory_space_constraint(wall, pltpu.VMEM))
    return new_state.reshape(state.shape), wall


def solution(mesh):
    return jax.shard_map(
        functools.partial(local, mesh.shape["wall"], mesh.shape["azim"]),
        mesh=mesh,
        in_specs=(P(None, "case", "wall", "azim"), P("case", "wall", "azim"), P(), P(), P(), P()),
        out_specs=(P(None, "case", "wall", "azim"), P("case", "azim")),
        check_vma=False,
    )
```
